32 devices in a mesh: groups: 2 (over y), seq: 4 (over z), dp: 2 (over x), strand: 2 (over core).
Axes of the slice: x: 2, y: 2, z: 4, core: 2. Of those that a mesh axis runs over, the one named last changes fastest.
Arguments:
- tokens: int32 [4, 2048], P(('groups', 'dp'), 'seq'), parts along dimension 0, may hold values from 0 to 3
- stem_table: bfloat16 [15, 4, 1536], replicated, may hold values from -1.5 to 1.5
- conv_weight: bfloat16 [3, 1536, 768], P(None, 'dp'), may hold values from -0.09375 to 0.09375
- gain_in: float32 [1536], replicated, may hold values from 0.1 to 1.9
- gain_mid: float32 [768], replicated, may hold values from 0.1 to 1.9
- point_weight: bfloat16 [768, 1536], P('dp'), may hold values from -0.21875 to 0.21875
Outputs:
- embedding: bfloat16 [4, 2048, 1536], P(('groups', 'dp'), 'seq', 'strand'), parts along dimension 0
The draws below stay inside these ranges and needn't reach their ends.
There are 2 independent parts, one for each index of `groups`. The reference program is written for one: setup_inputs(seed, part) draws one part's arguments, and reference() takes and returns one part's arrays. A program takes and returns all parts, laid end to end along the dimension named above; an argument that names none is the same for every part. Nothing has to cross between parts.
All inputs are finite; a program needn't handle non-finite values.
Results may differ from the reference program's by a relative error of at most 0.009.
Values may be sent and summed in bfloat16 or wider, within the bound.
A program may use at most 64 MiB of HBM per device.

```python
import jax
import jax.numpy as jnp
from jax import lax

C = 1536
H = 768
TAPS = 15
BASES = 4
DILATION_STEP = 256
BATCH = 2
LENGTH = 2048


def set_ends(result, rng, low, top_value):
    longest = result.shape.index(max(result.shape))
    spots = []
    for shift in (0, 1):
        where = [jax.random.randint(jax.random.fold_in(rng, axis), (), 0, length) for axis, length in enumerate(result.shape)]
        where[longest] = (where[longest] + shift) % result.shape[longest]
        spots.append(tuple(where))
    return result.at[spots[0]].set(low).at[spots[1]].set(top_value)


def shard_levels(key, shape, split, least, high):
    level = 1.0
    for dim, shards_of in split:
        heights = jax.random.uniform(jax.random.fold_in(jax.random.fold_in(key, 6), dim), (shards_of,), jnp.float32, least / len(split), high / len(split))
        level = level * jnp.repeat(jnp.exp(heights), shape[dim] // shards_of).reshape((-1,) + (1,) * (len(shape) - 1 - dim))
    return level


def scatter_about(stream_key, shape, width, limit, cuts=(), kind=jnp.bfloat16):
    entries = jax.random.normal(stream_key, shape, jnp.float32) * width
    if len(cuts) > 0:
        entries = shard_levels(stream_key, shape, cuts, -0.22, 0.18) * entries
    return jnp.clip(entries, min=-limit, max=limit).astype(kind)


def setup_inputs(seed: int = 0, part: int = 0) -> dict:
    key_list = jax.random.split(jax.random.key(seed), 7)
    part_keys = jax.random.split(jax.random.fold_in(key_list[6], part), 7)
    return {
        "tokens": set_ends(jax.random.randint(part_keys[0], (BATCH, LENGTH), 0, 4), jax.random.fold_in(part_keys[0], 1), 0, 3).astype(jnp.int32),
        "stem_table": scatter_about(key_list[1], (TAPS, BASES, C), TAPS ** -0.5, 1.5),
        "conv_weight": scatter_about(key_list[2], (3, C, H), (3 * C) ** -0.5, 0.09375, ((1, 2),)),
        "gain_in": jnp.clip(1.0 + 0.18 * jax.random.normal(key_list[3], (C,), jnp.float32), 0.1, 1.9),
        "gain_mid": jnp.clip(1.0 + 0.18 * jax.random.normal(key_list[4], (H,), jnp.float32), 0.1, 1.9),
        "point_weight": scatter_about(key_list[5], (H, C), H ** -0.5, 0.21875, ((0, 2),)),
    }


def normalize(values, gain):
    scale = lax.rsqrt(lax.optimization_barrier(jnp.mean(values * values, axis=-1, keepdims=True)) + 1e-06)
    return jax.nn.gelu(values * scale * gain.astype(jnp.float32))

def network(base_ids, stem_table, conv_weight, gain_in, gain_mid, point_weight):
    sequence_length = base_ids.shape[0]
    rim_width = TAPS // 2
    onehot = (base_ids[:, None] == jnp.arange(BASES, dtype=jnp.int32)[None, :]).astype(jnp.bfloat16)
    padded_hot = jnp.pad(onehot, ((rim_width, rim_width), (0, 0)))
    windows = jnp.concatenate([padded_hot[tap_position:tap_position + sequence_length] for tap_position in range(TAPS)], axis=1)
    embedded = jnp.dot(windows, stem_table.reshape(TAPS * BASES, C), preferred_element_type=jnp.float32).astype(jnp.bfloat16)
    stream = embedded.astype(jnp.float32)
    gelu_output = normalize(stream, gain_in).astype(jnp.bfloat16)
    padded_activation = jnp.pad(gelu_output, ((DILATION_STEP, DILATION_STEP), (0, 0)))
    conv_out = jnp.zeros((sequence_length, H), jnp.float32)
    for tap_position in range(3):
        tap_slices = padded_activation[tap_position * DILATION_STEP:tap_position * DILATION_STEP + sequence_length]
        conv_out = conv_out + jnp.dot(tap_slices, conv_weight[tap_position], preferred_element_type=jnp.float32)
    middle = normalize(conv_out, gain_mid).astype(jnp.bfloat16)
    branch = jnp.dot(middle, point_weight, preferred_element_type=jnp.float32)
    return (stream + branch).astype(jnp.bfloat16)

def reference(tokens, stem_table, conv_weight, gain_in, gain_mid, point_weight):

    def one_sequence(base_ids):
        forward = network(base_ids, stem_table, conv_weight, gain_in, gain_mid, point_weight)
        reverse_out = network(3 - base_ids[::-1], stem_table, conv_weight, gain_in, gain_mid, point_weight)
        total = forward.astype(jnp.float32) + reverse_out[::-1].astype(jnp.float32)
        return (total * 0.5).astype(jnp.bfloat16)
    return lax.map(one_sequence, tokens)
```

```python
import functools

import jax
import jax.numpy as jnp
from jax import lax
from jax.experimental import pallas as pl
from jax.experimental.pallas import tpu as pltpu
from jax.sharding import PartitionSpec as P

DILATION_STEP = 256
TAP_ROWS = 16
PIECE = 128
MESH = pl.DeviceIdType.MESH


def gelu(x):
    inner = x * (0.7978845608028654 + 0.035677408136300125 * (x * x))
    half = 0.5 * x
    return half + half * jnp.tanh(inner)


def dot_rows(a, b):
    return lax.dot_general(a, b, (((0,), (0,)), ((), ())), preferred_element_type=jnp.float32)


def kernel(
    counts, taps, tok_ref, table_ref, local_table_ref, gain_ref, gain_mid_ref, conv_ref, point_ref, out_ref,
    tok_buf, hot, scaled, act, conv_buf, point_buf, send_buf, recv_buf, own, mid, mid_in,
    tok_send, tok_recv, load_sem, point_load_sem, point_send, point_recv, fwd_send, fwd_recv,
    part_send, part_recv, mid_send, mid_recv,
):
    groups, seq, dp = counts
    rows = tok_ref.shape[1]
    width = table_ref.shape[1]
    depth = conv_ref.shape[1]
    inner = conv_ref.shape[2]
    point_rows = point_ref.shape[0]
    half = width // 2
    span = rows + 2 * DILATION_STEP
    pieces = rows // PIECE
    g = lax.axis_index("groups")
    s = lax.axis_index("seq")
    d = lax.axis_index("dp")
    c = lax.axis_index("strand")

    load_conv = pltpu.make_async_copy(conv_ref, conv_buf, load_sem)
    load_conv.start()
    col = pl.ds(pl.multiple_of(c * half, 128), half)
    load_point = pltpu.make_async_copy(
        point_ref.at[:, col], point_buf.at[pl.ds(pl.multiple_of(d * point_rows, 16), point_rows)], point_load_sem
    )
    load_point.start()

    barrier = pltpu.get_barrier_semaphore()

    def greet(target):
        pl.semaphore_signal(barrier, inc=1, device_id=target, device_id_type=MESH)

    for off in range(dp):
        j = lax.rem(d + off, dp)
        if off:
            greet((g, s, j, c))

        @pl.when(s > 0)
        def _():
            greet((g, s - 1, j, c))

        @pl.when(s < seq - 1)
        def _():
            greet((g, s + 1, j, c))

    greet((g, s, d, 1 - c))
    for goff in range(1, groups):
        greet((lax.rem(g + goff, groups), s, d, c))
    sides = 1 + (s > 0).astype(jnp.int32) + (s < seq - 1).astype(jnp.int32)
    pl.semaphore_wait(barrier, dp * sides - 1 + 1 + groups - 1)

    def tok_copy(off, place):
        j = lax.rem(d + off, dp)
        return pltpu.make_async_remote_copy(
            src_ref=tok_ref, dst_ref=tok_buf.at[off, 2 - place],
            send_sem=tok_send.at[off, 2 - place], recv_sem=tok_recv.at[off, 2 - place],
            device_id=(g, s + place - 1, j, c), device_id_type=MESH,
        )

    def tok_each(off, action):
        @pl.when(s > 0)
        def _():
            action(off, 0)

        @pl.when(s < seq - 1)
        def _():
            action(off, 2)

        if off:
            action(off, 1)

    for off in list(range(1, dp)) + [0]:
        tok_each(off, lambda o, p: tok_copy(o, p).start())
    tok_buf[0, 1] = tok_ref[...]
    for off in range(dp):
        @pl.when(s == 0)
        def _():
            tok_buf[off, 0] = jnp.full((1, rows), 4, jnp.int32)

        @pl.when(s == seq - 1)
        def _():
            tok_buf[off, 2] = jnp.full((1, rows), 4, jnp.int32)

    share = point_rows // groups

    def point_copy(off):
        j = lax.rem(d + off, dp)
        return pltpu.make_async_remote_copy(
            src_ref=point_ref.at[pl.ds(pl.multiple_of(g * share, 16), share), col],
            dst_ref=point_buf.at[pl.ds(pl.multiple_of(d * point_rows + g * share, 16), share)],
            send_sem=point_send.at[off - 1], recv_sem=point_recv.at[off - 1],
            device_id=(g, s, j, c), device_id_type=MESH,
        )

    def pass_copy(off, goff):
        source = lax.rem(d + dp - off, dp)
        block = point_buf.at[pl.ds(pl.multiple_of(source * point_rows + g * share, 16), share)]
        return pltpu.make_async_remote_copy(
            src_ref=block, dst_ref=block,
            send_sem=fwd_send.at[off - 1, goff - 1], recv_sem=fwd_recv.at[off - 1, goff - 1],
            device_id=(lax.rem(g + goff, groups), s, d, c), device_id_type=MESH,
        )

    for off in range(1, dp):
        point_copy(off).start()

    def tok_wait(off):
        def wait_from(o, p):
            pltpu.make_async_remote_copy(
                src_ref=tok_ref, dst_ref=tok_buf.at[o, p],
                send_sem=tok_send.at[o, p], recv_sem=tok_recv.at[o, p],
                device_id=(g, s, d, 1 - c), device_id_type=MESH,
            ).wait_recv()

        tok_each(off, wait_from)

    strand_rows = pl.ds(pl.multiple_of(c * 64, 64), 64)

    def make_act(slot):
        line = jnp.concatenate([tok_buf[slot, 0], tok_buf[slot, 1], tok_buf[slot, 2]], axis=1)
        wide = jnp.broadcast_to(line, (TAP_ROWS, 3 * rows))
        start = rows - DILATION_STEP - taps // 2 + TAP_ROWS - 1
        turned = pltpu.roll(wide, 3 * rows - start, 1, stride=1, stride_axis=0)[:, :span]
        place = lax.broadcasted_iota(jnp.int32, (TAP_ROWS, span), 1) + s * rows - DILATION_STEP
        turned = jnp.where((place >= 0) & (place < seq * rows), turned, 4)
        onehot = jnp.concatenate([jnp.where(turned == kind, 1.0, 0.0) for kind in range(4)], axis=0)
        low = onehot.astype(jnp.bfloat16)
        hot[...] = low
        total = jnp.zeros((1, span), jnp.float32)
        step = 256
        for at in range(0, width, step):
            e = dot_rows(table_ref[strand_rows, at : at + step], low)
            total = total + jnp.sum(e * e, axis=0, keepdims=True)
        scale = lax.rsqrt(total * (1.0 / width) + 1e-06)
        scale_high = scale.astype(jnp.bfloat16).astype(jnp.float32)
        scaled[0:64] = (onehot * scale_high).astype(jnp.bfloat16)
        scaled[64:128] = (onehot * (scale - scale_high)).astype(jnp.bfloat16)

    def act_block(at, size):
        z = dot_rows(scaled[:, at : at + size], local_table_ref[...])
        act[at : at + size, :] = gelu(z * gain_ref[...]).astype(jnp.bfloat16)

    def conv_block(at, size):
        total = jnp.zeros((size, inner), jnp.float32)
        for k in range(3):
            tap = jnp.where(c == 1, 2 - k, k)
            total = total + jnp.dot(
                act[at + k * DILATION_STEP : at + k * DILATION_STEP + size, :], conv_buf[tap],
                preferred_element_type=jnp.float32,
            )
        return total

    def part_copy(off, piece):
        j = lax.rem(d + off, dp)
        return pltpu.make_async_remote_copy(
            src_ref=send_buf.at[off - 1, piece], dst_ref=recv_buf.at[off - 1, piece],
            send_sem=part_send.at[off - 1, piece], recv_sem=part_recv.at[off - 1, piece],
            device_id=(g, s, j, c), device_id_type=MESH,
        )

    big = DILATION_STEP
    load_conv.wait()
    for off in range(1, dp):
        tok_wait(dp - off)
        make_act(dp - off)
        for at in range(0, 2 * DILATION_STEP, big):
            act_block(at, big)
        for at in range(0, rows, big):
            act_block(at + 2 * DILATION_STEP, big)
            total = conv_block(at, big).astype(jnp.bfloat16)
            for piece in range(at // PIECE, (at + big) // PIECE):
                send_buf[off - 1, piece] = total[piece * PIECE - at : piece * PIECE - at + PIECE]
                part_copy(off, piece).start()

    tok_wait(0)
    make_act(0)
    for at in range(0, 2 * DILATION_STEP, big):
        act_block(at, big)
    for off in range(1, dp):
        point_copy(off).wait_recv()
        for goff in range(1, groups):
            pass_copy(off, goff).start()
    for at in range(0, rows, big):
        act_block(at + 2 * DILATION_STEP, big)
        own[at : at + big] = conv_block(at, big)

    load_point.wait()
    for off in range(1, dp):
        for goff in range(1, groups):
            source = lax.rem(d + dp - off, dp)
            from_group = lax.rem(g + groups - goff, groups)
            block = point_buf.at[pl.ds(pl.multiple_of(source * point_rows + from_group * share, 16), share)]
            pltpu.make_async_remote_copy(
                src_ref=block, dst_ref=block,
                send_sem=fwd_send.at[off - 1, goff - 1], recv_sem=fwd_recv.at[off - 1, goff - 1],
                device_id=(lax.rem(g + goff, groups), s, d, c), device_id_type=MESH,
            ).wait_recv()

    def mid_copy(piece):
        return pltpu.make_async_remote_copy(
            src_ref=mid.at[piece], dst_ref=mid_in.at[piece],
            send_sem=mid_send.at[piece], recv_sem=mid_recv.at[piece],
            device_id=(g, s, d, 1 - c), device_id_type=MESH,
        )

    def finish(piece):
        at = piece * PIECE
        lanes = hot[:, DILATION_STEP + at : DILATION_STEP + at + PIECE]
        e = dot_rows(jnp.concatenate([lanes, lanes], axis=0), table_ref[:, col])
        mid_copy(piece).wait_recv()
        both = (mid[piece].astype(jnp.float32) + mid_in[piece].astype(jnp.float32)).astype(jnp.bfloat16)
        branch = jnp.dot(both, point_buf[...], preferred_element_type=jnp.float32)
        out_ref[0, at : at + PIECE, :] = ((e + branch) * 0.5).astype(jnp.bfloat16)

    for piece in range(pieces):
        x = own[piece * PIECE : (piece + 1) * PIECE]
        for off in range(1, dp):
            part_copy(off, piece).wait_recv()
            x = x + recv_buf[off - 1, piece].astype(jnp.float32)
        scale = lax.rsqrt(jnp.mean(x * x, axis=1, keepdims=True) + 1e-06)
        mid[piece] = gelu(x * scale * gain_mid_ref[...]).astype(jnp.bfloat16)
        mid_copy(piece).start()
        if piece:
            finish(piece - 1)
    finish(pieces - 1)

    for off in range(dp):
        tok_each(off, lambda o, p: tok_copy(o, p).wait_send())
    for off in range(1, dp):
        point_copy(off).wait_send()
        for goff in range(1, groups):
            pass_copy(off, goff).wait_send()
        for piece in range(pieces):
            part_copy(off, piece).wait_send()
    for piece in range(pieces):
        mid_copy(piece).wait_send()


def per_device(counts, tokens, stem_table, conv_weight, gain_in, gain_mid, point_weight):
    groups, seq, dp = counts
    rows = tokens.shape[1]
    taps, kinds, width = stem_table.shape
    depth, inner = conv_weight.shape[1:]
    half = width // 2
    pieces = rows // PIECE
    span = rows + 2 * DILATION_STEP
    d = lax.axis_index("dp")
    c = lax.axis_index("strand")
    gap = jnp.zeros((kinds, TAP_ROWS - taps, width), stem_table.dtype)
    by_kind = stem_table.transpose(1, 0, 2)
    ahead = jnp.concatenate([gap, by_kind[:, ::-1]], axis=1).reshape(kinds * TAP_ROWS, width)
    behind = jnp.concatenate([gap, by_kind[::-1]], axis=1).reshape(kinds * TAP_ROWS, width)
    table = jnp.concatenate([ahead, behind], axis=0)
    local = lax.dynamic_slice(jnp.where(c == 1, behind, ahead), (0, d * depth), (64, depth))
    local = jnp.concatenate([local, local], axis=0)
    gain_local = lax.dynamic_slice(gain_in, (d * depth,), (depth,))[None]
    vmem = pl.BlockSpec(memory_space=pltpu.VMEM)
    anywhere = pl.BlockSpec(memory_space=pl.ANY)
    dma = pltpu.SemaphoreType.DMA
    bf16 = jnp.bfloat16
    others, passes = max(dp - 1, 1), max(groups - 1, 1)
    return pl.pallas_call(
        functools.partial(kernel, counts, taps),
        out_shape=jax.ShapeDtypeStruct((1, rows, half), bf16),
        in_specs=[vmem] * 5 + [anywhere] * 2,
        out_specs=vmem,
        scratch_shapes=[
            pltpu.VMEM((dp, 3, 1, rows), jnp.int32),
            pltpu.VMEM((64, span), bf16),
            pltpu.VMEM((128, span), bf16),
            pltpu.VMEM((span, depth), bf16),
            pltpu.VMEM((3, depth, inner), bf16),
            pltpu.VMEM((inner, half), bf16),
            pltpu.VMEM((others, pieces, PIECE, inner), bf16),
            pltpu.VMEM((others, pieces, PIECE, inner), bf16),
            pltpu.VMEM((rows, inner), jnp.float32),
            pltpu.VMEM((pieces, PIECE, inner), bf16),
            pltpu.VMEM((pieces, PIECE, inner), bf16),
            dma((dp, 3)), dma((dp, 3)), dma, dma,
            dma((others,)), dma((others,)), dma((others, passes)), dma((others, passes)),
            dma((others, pieces)), dma((others, pieces)), dma((pieces,)), dma((pieces,)),
        ],
        compiler_params=pltpu.CompilerParams(
            collective_id=0, has_side_effects=True, vmem_limit_bytes=48 * 1024 * 1024
        ),
        cost_estimate=pl.CostEstimate(
            flops=2 * rows * inner * (3 * width + width), bytes_accessed=8 * 2**20,
            transcendentals=rows * width,
        ),
    )(tokens, table, local, gain_local, gain_mid[None], conv_weight, point_weight)


def solution(mesh):
    counts = tuple(mesh.shape[name] for name in ("groups", "seq", "dp"))
    return jax.shard_map(
        functools.partial(per_device, counts),
        mesh=mesh,
        in_specs=(P(("groups", "dp"), "seq"), P(), P(None, "dp", None), P(), P(), P("dp", None)),
        out_specs=P(("groups", "dp"), "seq", "strand"),
        check_vma=False,
    )
```

```python
import functools

import jax
import jax.numpy as jnp
from jax import lax
from jax.experimental import pallas as pl
from jax.experimental.pallas import tpu as pltpu
from jax.sharding import PartitionSpec as P

DILATION_STEP = 256
TAP_ROWS = 16
PIECE = 128
MESH = pl.DeviceIdType.MESH


def gelu(x):
    inner = x * (0.7978845608028654 + 0.035677408136300125 * (x * x))
    half = 0.5 * x
    return half + half * jnp.tanh(inner)


def dot_rows(a, b):
    return lax.dot_general(a, b, (((0,), (0,)), ((), ())), preferred_element_type=jnp.float32)


def kernel(
    counts, tok_ref, stem_ref, gain_ref, gain_mid_ref, conv_ref, point_ref, out_ref,
    stem_buf, table_ref, local_table_ref, local_gain_ref, tok_buf, hot, scaled, act, conv_buf, point_buf, send_buf, recv_buf, own, mid, mid_in,
    tok_send, tok_recv, load_sem, point_load_sem, point_send, point_recv, fwd_send, fwd_recv,
    part_send, part_recv, mid_send, mid_recv, out_buf, out_sem,
):
    groups, seq, dp = counts
    rows = tok_ref.shape[1]
    taps, kinds, width = stem_ref.shape
    depth = conv_ref.shape[1]
    inner = conv_ref.shape[2]
    point_rows = point_ref.shape[0]
    half = width // 2
    span = rows + 2 * DILATION_STEP
    pieces = rows // PIECE
    g = lax.axis_index("groups")
    s = lax.axis_index("seq")
    d = lax.axis_index("dp")
    c = lax.axis_index("strand")

    load_conv = pltpu.make_async_copy(conv_ref, conv_buf, load_sem)
    load_conv.start()
    col = pl.ds(pl.multiple_of(c * half, 128), half)
    load_point = pltpu.make_async_copy(
        point_ref.at[:, col], point_buf.at[pl.ds(pl.multiple_of(d * point_rows, 16), point_rows)], point_load_sem
    )
    load_point.start()

    barrier = pltpu.get_barrier_semaphore()

    def greet(target):
        pl.semaphore_signal(barrier, inc=1, device_id=target, device_id_type=MESH)

    for off in range(dp):
        j = lax.rem(d + off, dp)
        if off:
            greet((g, s, j, c))

        @pl.when(s > 0)
        def _():
            greet((g, s - 1, j, c))

        @pl.when(s < seq - 1)
        def _():
            greet((g, s + 1, j, c))

    greet((g, s, d, 1 - c))
    for goff in range(1, groups):
        greet((lax.rem(g + goff, groups), s, d, c))
    sides = 1 + (s > 0).astype(jnp.int32) + (s < seq - 1).astype(jnp.int32)
    pl.semaphore_wait(barrier, dp * sides - 1 + 1 + groups - 1)

    def tok_copy(off, place):
        j = lax.rem(d + off, dp)
        return pltpu.make_async_remote_copy(
            src_ref=tok_ref, dst_ref=tok_buf.at[off, 2 - place],
            send_sem=tok_send.at[off, 2 - place], recv_sem=tok_recv.at[off, 2 - place],
            device_id=(g, s + place - 1, j, c), device_id_type=MESH,
        )

    def tok_each(off, action):
        @pl.when(s > 0)
        def _():
            action(off, 0)

        @pl.when(s < seq - 1)
        def _():
            action(off, 2)

        if off:
            action(off, 1)

    for off in list(range(1, dp)) + [0]:
        tok_each(off, lambda o, p: tok_copy(o, p).start())
    tok_buf[0, 1] = tok_ref[...]
    for off in range(dp):
        @pl.when(s == 0)
        def _():
            tok_buf[off, 0] = jnp.full((1, rows), 4, jnp.int32)

        @pl.when(s == seq - 1)
        def _():
            tok_buf[off, 2] = jnp.full((1, rows), 4, jnp.int32)

    share = point_rows // groups

    def point_copy(off):
        j = lax.rem(d + off, dp)
        return pltpu.make_async_remote_copy(
            src_ref=point_ref.at[pl.ds(pl.multiple_of(g * share, 16), share), col],
            dst_ref=point_buf.at[pl.ds(pl.multiple_of(d * point_rows + g * share, 16), share)],
            send_sem=point_send.at[off - 1], recv_sem=point_recv.at[off - 1],
            device_id=(g, s, j, c), device_id_type=MESH,
        )

    def pass_copy(off, goff):
        source = lax.rem(d + dp - off, dp)
        block = point_buf.at[pl.ds(pl.multiple_of(source * point_rows + g * share, 16), share)]
        return pltpu.make_async_remote_copy(
            src_ref=block, dst_ref=block,
            send_sem=fwd_send.at[off - 1, goff - 1], recv_sem=fwd_recv.at[off - 1, goff - 1],
            device_id=(lax.rem(g + goff, groups), s, d, c), device_id_type=MESH,
        )

    for off in range(1, dp):
        point_copy(off).start()

    def tok_wait(off):
        def wait_from(o, p):
            pltpu.make_async_remote_copy(
                src_ref=tok_ref, dst_ref=tok_buf.at[o, p],
                send_sem=tok_send.at[o, p], recv_sem=tok_recv.at[o, p],
                device_id=(g, s, d, 1 - c), device_id_type=MESH,
            ).wait_recv()

        tok_each(off, wait_from)

    stem_buf[...] = jnp.zeros_like(stem_buf)
    for tap in range(taps):
        stem_buf[tap * kinds : (tap + 1) * kinds] = stem_ref[tap].astype(jnp.float32)
    row = lax.broadcasted_iota(jnp.int32, (128, 64), 0)
    source = lax.broadcasted_iota(jnp.int32, (128, 64), 1)
    place = row % TAP_ROWS
    kind = (row // TAP_ROWS) % kinds
    ahead = kinds * (TAP_ROWS - 1 - place) + kind
    behind = kinds * (place - 1) + kinds - 1 - kind
    pick = (source == jnp.where(row < 64, ahead, behind)) & (place > 0)
    pick = jnp.where(pick, 1.0, 0.0).astype(jnp.bfloat16)
    table_ref[...] = jnp.dot(
        pick, stem_buf[...].astype(jnp.bfloat16), preferred_element_type=jnp.float32
    ).astype(jnp.bfloat16)
    strand_rows = pl.ds(pl.multiple_of(c * 64, 64), 64)
    for j in range(dp):
        @pl.when(d == j)
        def _():
            block = table_ref[strand_rows, j * depth : (j + 1) * depth]
            local_table_ref[0:64] = block
            local_table_ref[64:128] = block
            local_gain_ref[...] = gain_ref[...].reshape(1, width)[:, j * depth : (j + 1) * depth]

    strand_rows = pl.ds(pl.multiple_of(c * 64, 64), 64)

    def make_act(slot):
        line = jnp.concatenate([tok_buf[slot, 0], tok_buf[slot, 1], tok_buf[slot, 2]], axis=1)
        wide = jnp.broadcast_to(line, (TAP_ROWS, 3 * rows))
        start = rows - DILATION_STEP - taps // 2 + TAP_ROWS - 1
        turned = pltpu.roll(wide, 3 * rows - start, 1, stride=1, stride_axis=0)[:, :span]
        place = lax.broadcasted_iota(jnp.int32, (TAP_ROWS, span), 1) + s * rows - DILATION_STEP
        turned = jnp.where((place >= 0) & (place < seq * rows), turned, 4)
        onehot = jnp.concatenate([jnp.where(turned == kind, 1.0, 0.0) for kind in range(4)], axis=0)
        low = onehot.astype(jnp.bfloat16)
        hot[...] = low
        total = jnp.zeros((1, span), jnp.float32)
        step = 256
        for at in range(0, width, step):
            e = dot_rows(table_ref[strand_rows, at : at + step], low)
            total = total + jnp.sum(e * e, axis=0, keepdims=True)
        scale = lax.rsqrt(total * (1.0 / width) + 1e-06)
        scale_high = scale.astype(jnp.bfloat16).astype(jnp.float32)
        scaled[0:64] = (onehot * scale_high).astype(jnp.bfloat16)
        scaled[64:128] = (onehot * (scale - scale_high)).astype(jnp.bfloat16)

    def act_block(at, size):
        z = dot_rows(scaled[:, at : at + size], local_table_ref[...])
        act[at : at + size, :] = gelu(z * local_gain_ref[...]).astype(jnp.bfloat16)

    def conv_block(at, size):
        total = jnp.zeros((size, inner), jnp.float32)
        for k in range(3):
            tap = jnp.where(c == 1, 2 - k, k)
            total = total + jnp.dot(
                act[at + k * DILATION_STEP : at + k * DILATION_STEP + size, :], conv_buf[tap],
                preferred_element_type=jnp.float32,
            )
        return total

    def part_copy(off, piece):
        j = lax.rem(d + off, dp)
        return pltpu.make_async_remote_copy(
            src_ref=send_buf.at[off - 1, piece], dst_ref=recv_buf.at[off - 1, piece],
            send_sem=part_send.at[off - 1, piece], recv_sem=part_recv.at[off - 1, piece],
            device_id=(g, s, j, c), device_id_type=MESH,
        )

    big = DILATION_STEP
    load_conv.wait()
    for off in range(1, dp):
        tok_wait(dp - off)
        make_act(dp - off)
        for at in range(0, 2 * DILATION_STEP, big):
            act_block(at, big)
        for at in range(0, rows, big):
            act_block(at + 2 * DILATION_STEP, big)
            total = conv_block(at, big).astype(jnp.bfloat16)
            for piece in range(at // PIECE, (at + big) // PIECE):
                send_buf[off - 1, piece] = total[piece * PIECE - at : piece * PIECE - at + PIECE]
                part_copy(off, piece).start()

    tok_wait(0)
    make_act(0)
    for at in range(0, 2 * DILATION_STEP, big):
        act_block(at, big)
    for off in range(1, dp):
        point_copy(off).wait_recv()
        for goff in range(1, groups):
            pass_copy(off, goff).start()
    for at in range(0, rows, big):
        act_block(at + 2 * DILATION_STEP, big)
        own[at : at + big] = conv_block(at, big)

    load_point.wait()
    for off in range(1, dp):
        for goff in range(1, groups):
            source = lax.rem(d + dp - off, dp)
            from_group = lax.rem(g + groups - goff, groups)
            block = point_buf.at[pl.ds(pl.multiple_of(source * point_rows + from_group * share, 16), share)]
            pltpu.make_async_remote_copy(
                src_ref=block, dst_ref=block,
                send_sem=fwd_send.at[off - 1, goff - 1], recv_sem=fwd_recv.at[off - 1, goff - 1],
                device_id=(lax.rem(g + goff, groups), s, d, c), device_id_type=MESH,
            ).wait_recv()

    def mid_copy(piece):
        return pltpu.make_async_remote_copy(
            src_ref=mid.at[piece], dst_ref=mid_in.at[piece],
            send_sem=mid_send.at[piece], recv_sem=mid_recv.at[piece],
            device_id=(g, s, d, 1 - c), device_id_type=MESH,
        )

    def out_copy(piece):
        block = pl.ds(piece * PIECE, PIECE)
        return pltpu.make_async_copy(out_buf.at[block], out_ref.at[0, block], out_sem.at[piece])

    def finish(piece):
        at = piece * PIECE
        lanes = hot[:, DILATION_STEP + at : DILATION_STEP + at + PIECE]
        e = dot_rows(jnp.concatenate([lanes, lanes], axis=0), table_ref[:, col])
        mid_copy(piece).wait_recv()
        both = (mid[piece].astype(jnp.float32) + mid_in[piece].astype(jnp.float32)).astype(jnp.bfloat16)
        branch = jnp.dot(both, point_buf[...], preferred_element_type=jnp.float32)
        out_buf[at : at + PIECE, :] = ((e + branch) * 0.5).astype(jnp.bfloat16)
        out_copy(piece).start()

    for piece in range(pieces):
        x = own[piece * PIECE : (piece + 1) * PIECE]
        for off in range(1, dp):
            part_copy(off, piece).wait_recv()
            x = x + recv_buf[off - 1, piece].astype(jnp.float32)
        scale = lax.rsqrt(jnp.mean(x * x, axis=1, keepdims=True) + 1e-06)
        mid[piece] = gelu(x * scale * gain_mid_ref[...].reshape(1, inner)).astype(jnp.bfloat16)
        mid_copy(piece).start()
        if piece:
            finish(piece - 1)
    finish(pieces - 1)

    for off in range(dp):
        tok_each(off, lambda o, p: tok_copy(o, p).wait_send())
    for off in range(1, dp):
        point_copy(off).wait_send()
        for goff in range(1, groups):
            pass_copy(off, goff).wait_send()
        for piece in range(pieces):
            part_copy(off, piece).wait_send()
    for piece in range(pieces):
        mid_copy(piece).wait_send()
        out_copy(piece).wait()


def per_device(counts, tokens, stem_table, conv_weight, gain_in, gain_mid, point_weight):
    groups, seq, dp = counts
    rows = tokens.shape[1]
    taps, kinds, width = stem_table.shape
    depth, inner = conv_weight.shape[1:]
    half = width // 2
    pieces = rows // PIECE
    span = rows + 2 * DILATION_STEP
    vmem = pl.BlockSpec(memory_space=pltpu.VMEM)
    anywhere = pl.BlockSpec(memory_space=pltpu.HBM)
    dma = pltpu.SemaphoreType.DMA
    bf16 = jnp.bfloat16
    others, passes = max(dp - 1, 1), max(groups - 1, 1)
    return pl.pallas_call(
        functools.partial(kernel, counts),
        out_shape=jax.ShapeDtypeStruct((1, rows, half), bf16),
        in_specs=[vmem] * 4 + [anywhere] * 2,
        out_specs=anywhere,
        scratch_shapes=[
            pltpu.VMEM((64, width), jnp.float32),
            pltpu.VMEM((128, width), bf16),
            pltpu.VMEM((128, depth), bf16),
            pltpu.VMEM((1, depth), jnp.float32),
            pltpu.VMEM((dp, 3, 1, rows), jnp.int32),
            pltpu.VMEM((64, span), bf16),
            pltpu.VMEM((128, span), bf16),
            pltpu.VMEM((span, depth), bf16),
            pltpu.VMEM((3, depth, inner), bf16),
            pltpu.VMEM((inner, half), bf16),
            pltpu.VMEM((others, pieces, PIECE, inner), bf16),
            pltpu.VMEM((others, pieces, PIECE, inner), bf16),
            pltpu.VMEM((rows, inner), jnp.float32),
            pltpu.VMEM((pieces, PIECE, inner), bf16),
            pltpu.VMEM((pieces, PIECE, inner), bf16),
            dma((dp, 3)), dma((dp, 3)), dma, dma,
            dma((others,)), dma((others,)), dma((others, passes)), dma((others, passes)),
            dma((others, pieces)), dma((others, pieces)), dma((pieces,)), dma((pieces,)),
            pltpu.VMEM((rows, half), bf16), dma((pieces,)),
        ],
        compiler_params=pltpu.CompilerParams(
            collective_id=0, has_side_effects=True, vmem_limit_bytes=60 * 1024 * 1024
        ),
        cost_estimate=pl.CostEstimate(
            flops=2 * rows * inner * (3 * width + width), bytes_accessed=8 * 2**20,
            transcendentals=rows * width,
        ),
    )(tokens, stem_table, gain_in, gain_mid, conv_weight, point_weight)


def solution(mesh):
    counts = tuple(mesh.shape[name] for name in ("groups", "seq", "dp"))
    return jax.shard_map(
        functools.partial(per_device, counts),
        mesh=mesh,
        in_specs=(P(("groups", "dp"), "seq"), P(), P(None, "dp", None), P(), P(), P("dp", None)),
        out_specs=P(("groups", "dp"), "seq", "strand"),
        check_vma=False,
    )
```

```python
import functools

import jax
import jax.numpy as jnp
from jax import lax
from jax.experimental import pallas as pl
from jax.experimental.pallas import tpu as pltpu
from jax.sharding import PartitionSpec as P

DILATION_STEP = 256
TAP_ROWS = 16
PIECE = 128
MESH = pl.DeviceIdType.MESH


def gelu(x):
    inner = x * (0.7978845608028654 + 0.035677408136300125 * (x * x))
    half = 0.5 * x
    return half + half * jnp.tanh(inner)


def dot_rows(a, b):
    return lax.dot_general(a, b, (((0,), (0,)), ((), ())), preferred_element_type=jnp.float32)


def kernel(
    counts, tok_ref, stem_ref, gain_ref, gain_mid_ref, conv_ref, point_ref, out_ref,
    stem_buf, table_ref, local_table_ref, local_gain_ref, tok_buf, hot, scaled, act, conv_buf, point_buf, send_buf, recv_buf, own, mid, mid_in,
    tok_send, tok_recv, load_sem, point_load_sem, point_send, point_recv, fwd_send, fwd_recv,
    part_send, part_recv, mid_send, mid_recv,
):
    groups, seq, dp = counts
    rows = tok_ref.shape[1]
    taps, kinds, width = stem_ref.shape
    depth = conv_ref.shape[1]
    inner = conv_ref.shape[2]
    point_rows = point_ref.shape[0]
    half = width // 2
    span = rows + 2 * DILATION_STEP
    pieces = rows // PIECE
    g = lax.axis_index("groups")
    s = lax.axis_index("seq")
    d = lax.axis_index("dp")
    c = lax.axis_index("strand")

    load_conv = pltpu.make_async_copy(conv_ref, conv_buf, load_sem)
    load_conv.start()
    col = pl.ds(pl.multiple_of(c * half, 128), half)
    load_point = pltpu.make_async_copy(
        point_ref.at[:, col], point_buf.at[pl.ds(pl.multiple_of(d * point_rows, 16), point_rows)], point_load_sem
    )
    load_point.start()

    barrier = pltpu.get_barrier_semaphore()

    def greet(target):
        pl.semaphore_signal(barrier, inc=1, device_id=target, device_id_type=MESH)

    for off in range(dp):
        j = lax.rem(d + off, dp)
        if off:
            greet((g, s, j, c))

        @pl.when(s > 0)
        def _():
            greet((g, s - 1, j, c))

        @pl.when(s < seq - 1)
        def _():
            greet((g, s + 1, j, c))

    greet((g, s, d, 1 - c))
    for goff in range(1, groups):
        greet((lax.rem(g + goff, groups), s, d, c))
    sides = 1 + (s > 0).astype(jnp.int32) + (s < seq - 1).astype(jnp.int32)
    pl.semaphore_wait(barrier, dp * sides - 1 + 1 + groups - 1)

    def tok_copy(off, place):
        j = lax.rem(d + off, dp)
        return pltpu.make_async_remote_copy(
            src_ref=tok_ref, dst_ref=tok_buf.at[off, 2 - place],
            send_sem=tok_send.at[off, 2 - place], recv_sem=tok_recv.at[off, 2 - place],
            device_id=(g, s + place - 1, j, c), device_id_type=MESH,
        )

    def tok_each(off, action):
        @pl.when(s > 0)
        def _():
            action(off, 0)

        @pl.when(s < seq - 1)
        def _():
            action(off, 2)

        if off:
            action(off, 1)

    for off in list(range(1, dp)) + [0]:
        tok_each(off, lambda o, p: tok_copy(o, p).start())
    tok_buf[0, 1] = tok_ref[...]
    for off in range(dp):
        @pl.when(s == 0)
        def _():
            tok_buf[off, 0] = jnp.full((1, rows), 4, jnp.int32)

        @pl.when(s == seq - 1)
        def _():
            tok_buf[off, 2] = jnp.full((1, rows), 4, jnp.int32)

    share = point_rows // groups

    def point_copy(off):
        j = lax.rem(d + off, dp)
        return pltpu.make_async_remote_copy(
            src_ref=point_ref.at[pl.ds(pl.multiple_of(g * share, 16), share), col],
            dst_ref=point_buf.at[pl.ds(pl.multiple_of(d * point_rows + g * share, 16), share)],
            send_sem=point_send.at[off - 1], recv_sem=point_recv.at[off - 1],
            device_id=(g, s, j, c), device_id_type=MESH,
        )

    def pass_copy(off, goff):
        source = lax.rem(d + dp - off, dp)
        block = point_buf.at[pl.ds(pl.multiple_of(source * point_rows + g * share, 16), share)]
        return pltpu.make_async_remote_copy(
            src_ref=block, dst_ref=block,
            send_sem=fwd_send.at[off - 1, goff - 1], recv_sem=fwd_recv.at[off - 1, goff - 1],
            device_id=(lax.rem(g + goff, groups), s, d, c), device_id_type=MESH,
        )

    for off in range(1, dp):
        point_copy(off).start()

    def tok_wait(off):
        def wait_from(o, p):
            pltpu.make_async_remote_copy(
                src_ref=tok_ref, dst_ref=tok_buf.at[o, p],
                send_sem=tok_send.at[o, p], recv_sem=tok_recv.at[o, p],
                device_id=(g, s, d, 1 - c), device_id_type=MESH,
            ).wait_recv()

        tok_each(off, wait_from)

    stem_buf[...] = jnp.zeros_like(stem_buf)
    for tap in range(taps):
        stem_buf[tap * kinds : (tap + 1) * kinds] = stem_ref[tap].astype(jnp.float32)
    row = lax.broadcasted_iota(jnp.int32, (128, 64), 0)
    source = lax.broadcasted_iota(jnp.int32, (128, 64), 1)
    place = row % TAP_ROWS
    kind = (row // TAP_ROWS) % kinds
    ahead = kinds * (TAP_ROWS - 1 - place) + kind
    behind = kinds * (place - 1) + kinds - 1 - kind
    pick = (source == jnp.where(row < 64, ahead, behind)) & (place > 0)
    pick = jnp.where(pick, 1.0, 0.0).astype(jnp.bfloat16)
    table_ref[...] = jnp.dot(
        pick, stem_buf[...].astype(jnp.bfloat16), preferred_element_type=jnp.float32
    ).astype(jnp.bfloat16)
    strand_rows = pl.ds(pl.multiple_of(c * 64, 64), 64)
    for j in range(dp):
        @pl.when(d == j)
        def _():
            block = table_ref[strand_rows, j * depth : (j + 1) * depth]
            local_table_ref[0:64] = block
            local_table_ref[64:128] = block
            local_gain_ref[...] = gain_ref[...].reshape(1, width)[:, j * depth : (j + 1) * depth]

    strand_rows = pl.ds(pl.multiple_of(c * 64, 64), 64)

    def make_act(slot):
        line = jnp.concatenate([tok_buf[slot, 0], tok_buf[slot, 1], tok_buf[slot, 2]], axis=1)
        wide = jnp.broadcast_to(line, (TAP_ROWS, 3 * rows))
        start = rows - DILATION_STEP - taps // 2 + TAP_ROWS - 1
        turned = pltpu.roll(wide, 3 * rows - start, 1, stride=1, stride_axis=0)[:, :span]
        place = lax.broadcasted_iota(jnp.int32, (TAP_ROWS, span), 1) + s * rows - DILATION_STEP
        turned = jnp.where((place >= 0) & (place < seq * rows), turned, 4)
        onehot = jnp.concatenate([jnp.where(turned == kind, 1.0, 0.0) for kind in range(4)], axis=0)
        low = onehot.astype(jnp.bfloat16)
        hot[...] = low
        total = jnp.zeros((1, span), jnp.float32)
        step = 256
        for at in range(0, width, step):
            e = dot_rows(table_ref[strand_rows, at : at + step], low)
            total = total + jnp.sum(e * e, axis=0, keepdims=True)
        scale = lax.rsqrt(total * (1.0 / width) + 1e-06)
        scale_high = scale.astype(jnp.bfloat16).astype(jnp.float32)
        scaled[0:64] = (onehot * scale_high).astype(jnp.bfloat16)
        scaled[64:128] = (onehot * (scale - scale_high)).astype(jnp.bfloat16)

    def act_block(at, size):
        z = dot_rows(scaled[:, at : at + size], local_table_ref[...])
        act[at : at + size, :] = gelu(z * local_gain_ref[...]).astype(jnp.bfloat16)

    def conv_block(at, size):
        total = jnp.zeros((size, inner), jnp.float32)
        for k in range(3):
            tap = jnp.where(c == 1, 2 - k, k)
            total = total + jnp.dot(
                act[at + k * DILATION_STEP : at + k * DILATION_STEP + size, :], conv_buf[tap],
                preferred_element_type=jnp.float32,
            )
        return total

    def part_copy(off, piece):
        j = lax.rem(d + off, dp)
        return pltpu.make_async_remote_copy(
            src_ref=send_buf.at[off - 1, piece], dst_ref=recv_buf.at[off - 1, piece],
            send_sem=part_send.at[off - 1, piece], recv_sem=part_recv.at[off - 1, piece],
            device_id=(g, s, j, c), device_id_type=MESH,
        )

    big = DILATION_STEP
    load_conv.wait()
    for off in range(1, dp):
        tok_wait(dp - off)
        make_act(dp - off)
        for at in range(0, 2 * DILATION_STEP, big):
            act_block(at, big)
        for at in range(0, rows, big):
            act_block(at + 2 * DILATION_STEP, big)
            total = conv_block(at, big).astype(jnp.bfloat16)
            for piece in range(at // PIECE, (at + big) // PIECE):
                send_buf[off - 1, piece] = total[piece * PIECE - at : piece * PIECE - at + PIECE]
                part_copy(off, piece).start()

    tok_wait(0)
    make_act(0)
    for at in range(0, 2 * DILATION_STEP, big):
        act_block(at, big)
    for off in range(1, dp):
        point_copy(off).wait_recv()
        for goff in range(1, groups):
            pass_copy(off, goff).start()
    for at in range(0, rows, big):
        act_block(at + 2 * DILATION_STEP, big)
        own[at : at + big] = conv_block(at, big)

    load_point.wait()
    for off in range(1, dp):
        for goff in range(1, groups):
            source = lax.rem(d + dp - off, dp)
            from_group = lax.rem(g + groups - goff, groups)
            block = point_buf.at[pl.ds(pl.multiple_of(source * point_rows + from_group * share, 16), share)]
            pltpu.make_async_remote_copy(
                src_ref=block, dst_ref=block,
                send_sem=fwd_send.at[off - 1, goff - 1], recv_sem=fwd_recv.at[off - 1, goff - 1],
                device_id=(lax.rem(g + goff, groups), s, d, c), device_id_type=MESH,
            ).wait_recv()

    def mid_copy(piece):
        return pltpu.make_async_remote_copy(
            src_ref=mid.at[piece], dst_ref=mid_in.at[piece],
            send_sem=mid_send.at[piece], recv_sem=mid_recv.at[piece],
            device_id=(g, s, d, 1 - c), device_id_type=MESH,
        )

    def finish(piece):
        at = piece * PIECE
        lanes = hot[:, DILATION_STEP + at : DILATION_STEP + at + PIECE]
        e = dot_rows(jnp.concatenate([lanes, lanes], axis=0), table_ref[:, col])
        mid_copy(piece).wait_recv()
        both = (mid[piece].astype(jnp.float32) + mid_in[piece].astype(jnp.float32)).astype(jnp.bfloat16)
        branch = jnp.dot(both, point_buf[...], preferred_element_type=jnp.float32)
        out_ref[0, at : at + PIECE, :] = ((e + branch) * 0.5).astype(jnp.bfloat16)

    for piece in range(pieces):
        x = own[piece * PIECE : (piece + 1) * PIECE]
        for off in range(1, dp):
            part_copy(off, piece).wait_recv()
            x = x + recv_buf[off - 1, piece].astype(jnp.float32)
        scale = lax.rsqrt(jnp.mean(x * x, axis=1, keepdims=True) + 1e-06)
        mid[piece] = gelu(x * scale * gain_mid_ref[...].reshape(1, inner)).astype(jnp.bfloat16)
        mid_copy(piece).start()
        if piece:
            finish(piece - 1)
    finish(pieces - 1)

    for off in range(dp):
        tok_each(off, lambda o, p: tok_copy(o, p).wait_send())
    for off in range(1, dp):
        point_copy(off).wait_send()
        for goff in range(1, groups):
            pass_copy(off, goff).wait_send()
        for piece in range(pieces):
            part_copy(off, piece).wait_send()
    for piece in range(pieces):
        mid_copy(piece).wait_send()


def per_device(counts, tokens, stem_table, conv_weight, gain_in, gain_mid, point_weight):
    groups, seq, dp = counts
    rows = tokens.shape[1]
    taps, kinds, width = stem_table.shape
    depth, inner = conv_weight.shape[1:]
    half = width // 2
    pieces = rows // PIECE
    span = rows + 2 * DILATION_STEP
    vmem = pl.BlockSpec(memory_space=pltpu.VMEM)
    anywhere = pl.BlockSpec(memory_space=pltpu.HBM)
    dma = pltpu.SemaphoreType.DMA
    bf16 = jnp.bfloat16
    others, passes = max(dp - 1, 1), max(groups - 1, 1)
    return pl.pallas_call(
        functools.partial(kernel, counts),
        out_shape=jax.ShapeDtypeStruct((1, rows, half), bf16),
        in_specs=[vmem] * 4 + [anywhere] * 2,
        out_specs=vmem,
        scratch_shapes=[
            pltpu.VMEM((64, width), jnp.float32),
            pltpu.VMEM((128, width), bf16),
            pltpu.VMEM((128, depth), bf16),
            pltpu.VMEM((1, depth), jnp.float32),
            pltpu.VMEM((dp, 3, 1, rows), jnp.int32),
            pltpu.VMEM((64, span), bf16),
            pltpu.VMEM((128, span), bf16),
            pltpu.VMEM((span, depth), bf16),
            pltpu.VMEM((3, depth, inner), bf16),
            pltpu.VMEM((inner, half), bf16),
            pltpu.VMEM((others, pieces, PIECE, inner), bf16),
            pltpu.VMEM((others, pieces, PIECE, inner), bf16),
            pltpu.VMEM((rows, inner), jnp.float32),
            pltpu.VMEM((pieces, PIECE, inner), bf16),
            pltpu.VMEM((pieces, PIECE, inner), bf16),
            dma((dp, 3)), dma((dp, 3)), dma, dma,
            dma((others,)), dma((others,)), dma((others, passes)), dma((others, passes)),
            dma((others, pieces)), dma((others, pieces)), dma((pieces,)), dma((pieces,)),
        ],
        compiler_params=pltpu.CompilerParams(
            collective_id=0, has_side_effects=True, vmem_limit_bytes=48 * 1024 * 1024
        ),
        cost_estimate=pl.CostEstimate(
            flops=2 * rows * inner * (3 * width + width), bytes_accessed=8 * 2**20,
            transcendentals=rows * width,
        ),
    )(tokens, stem_table, gain_in, gain_mid, conv_weight, point_weight)


def solution(mesh):
    counts = tuple(mesh.shape[name] for name in ("groups", "seq", "dp"))
    return jax.shard_map(
        functools.partial(per_device, counts),
        mesh=mesh,
        in_specs=(P(("groups", "dp"), "seq"), P(), P(None, "dp", None), P(), P(), P("dp", None)),
        out_specs=P(("groups", "dp"), "seq", "strand"),
        check_vma=False,
    )
```

```python
import functools

import jax
import jax.numpy as jnp
from jax import lax
from jax.experimental import pallas as pl
from jax.experimental.pallas import tpu as pltpu
from jax.sharding import PartitionSpec as P

DILATION_STEP = 256
TAP_ROWS = 16
PIECE = 128
MESH = pl.DeviceIdType.MESH


def gelu(x):
    inner = x * (0.7978845608028654 + 0.035677408136300125 * (x * x))
    half = 0.5 * x
    return half + half * jnp.tanh(inner)


def dot_rows(a, b):
    return lax.dot_general(a, b, (((0,), (0,)), ((), ())), preferred_element_type=jnp.float32)


def kernel(
    counts, tok_ref, stem_ref, gain_ref, gain_mid_ref, conv_ref, point_ref, out_ref,
    stem_buf, table_ref, local_table_ref, local_gain_ref, tok_buf, hot, scaled, act, conv_buf, point_buf, send_buf, recv_buf, own, mid, mid_in,
    tok_send, tok_recv, load_sem, point_load_sem, point_send, point_recv, fwd_send, fwd_recv,
    part_send, part_recv, mid_send, mid_recv, out_buf, out_sem,
):
    groups, seq, dp = counts
    rows = tok_ref.shape[1]
    taps, kinds, width = stem_ref.shape
    depth = conv_ref.shape[1]
    inner = conv_ref.shape[2]
    point_rows = point_ref.shape[0]
    half = width // 2
    span = rows + 2 * DILATION_STEP
    pieces = rows // PIECE
    g = lax.axis_index("groups")
    s = lax.axis_index("seq")
    d = lax.axis_index("dp")
    c = lax.axis_index("strand")

    load_conv = pltpu.make_async_copy(conv_ref, conv_buf, load_sem)
    load_conv.start()
    col = pl.ds(pl.multiple_of(c * half, 128), half)
    load_point = pltpu.make_async_copy(
        point_ref.at[:, col], point_buf.at[pl.ds(pl.multiple_of(d * point_rows, 16), point_rows)], point_load_sem
    )
    load_point.start()

    barrier = pltpu.get_barrier_semaphore()

    def greet(target):
        pl.semaphore_signal(barrier, inc=1, device_id=target, device_id_type=MESH)

    for off in range(dp):
        j = lax.rem(d + off, dp)
        if off:
            greet((g, s, j, c))

        @pl.when(s > 0)
        def _():
            greet((g, s - 1, j, c))

        @pl.when(s < seq - 1)
        def _():
            greet((g, s + 1, j, c))

    greet((g, s, d, 1 - c))
    for goff in range(1, groups):
        greet((lax.rem(g + goff, groups), s, d, c))
    sides = 1 + (s > 0).astype(jnp.int32) + (s < seq - 1).astype(jnp.int32)
    pl.semaphore_wait(barrier, dp * sides - 1 + 1 + groups - 1)

    def tok_copy(off, place):
        j = lax.rem(d + off, dp)
        return pltpu.make_async_remote_copy(
            src_ref=tok_ref, dst_ref=tok_buf.at[off, 2 - place],
            send_sem=tok_send.at[off, 2 - place], recv_sem=tok_recv.at[off, 2 - place],
            device_id=(g, s + place - 1, j, c), device_id_type=MESH,
        )

    def tok_each(off, action):
        @pl.when(s > 0)
        def _():
            action(off, 0)

        @pl.when(s < seq - 1)
        def _():
            action(off, 2)

        if off:
            action(off, 1)

    for off in list(range(1, dp)) + [0]:
        tok_each(off, lambda o, p: tok_copy(o, p).start())
    tok_buf[0, 1] = tok_ref[...]
    for off in range(dp):
        @pl.when(s == 0)
        def _():
            tok_buf[off, 0] = jnp.full((1, rows), 4, jnp.int32)

        @pl.when(s == seq - 1)
        def _():
            tok_buf[off, 2] = jnp.full((1, rows), 4, jnp.int32)

    share = point_rows // groups

    def point_copy(off):
        j = lax.rem(d + off, dp)
        return pltpu.make_async_remote_copy(
            src_ref=point_ref.at[pl.ds(pl.multiple_of(g * share, 16), share), col],
            dst_ref=point_buf.at[pl.ds(pl.multiple_of(d * point_rows + g * share, 16), share)],
            send_sem=point_send.at[off - 1], recv_sem=point_recv.at[off - 1],
            device_id=(g, s, j, c), device_id_type=MESH,
        )

    def pass_copy(off, goff):
        source = lax.rem(d + dp - off, dp)
        block = point_buf.at[pl.ds(pl.multiple_of(source * point_rows + g * share, 16), share)]
        return pltpu.make_async_remote_copy(
            src_ref=block, dst_ref=block,
            send_sem=fwd_send.at[off - 1, goff - 1], recv_sem=fwd_recv.at[off - 1, goff - 1],
            device_id=(lax.rem(g + goff, groups), s, d, c), device_id_type=MESH,
        )

    for off in range(1, dp):
        point_copy(off).start()

    def tok_wait(off):
        def wait_from(o, p):
            pltpu.make_async_remote_copy(
                src_ref=tok_ref, dst_ref=tok_buf.at[o, p],
                send_sem=tok_send.at[o, p], recv_sem=tok_recv.at[o, p],
                device_id=(g, s, d, 1 - c), device_id_type=MESH,
            ).wait_recv()

        tok_each(off, wait_from)

    stem_buf[...] = jnp.zeros_like(stem_buf)
    for tap in range(taps):
        stem_buf[tap * kinds : (tap + 1) * kinds] = stem_ref[tap].astype(jnp.float32)
    row = lax.broadcasted_iota(jnp.int32, (128, 64), 0)
    source = lax.broadcasted_iota(jnp.int32, (128, 64), 1)
    place = row % TAP_ROWS
    kind = (row // TAP_ROWS) % kinds
    ahead = kinds * (TAP_ROWS - 1 - place) + kind
    behind = kinds * (place - 1) + kinds - 1 - kind
    pick = (source == jnp.where(row < 64, ahead, behind)) & (place > 0)
    pick = jnp.where(pick, 1.0, 0.0).astype(jnp.bfloat16)
    table_ref[...] = jnp.dot(
        pick, stem_buf[...].astype(jnp.bfloat16), preferred_element_type=jnp.float32
    ).astype(jnp.bfloat16)
    strand_rows = pl.ds(pl.multiple_of(c * 64, 64), 64)
    for j in range(dp):
        @pl.when(d == j)
        def _():
            block = table_ref[strand_rows, j * depth : (j + 1) * depth]
            local_table_ref[0:64] = block
            local_table_ref[64:128] = block
            local_gain_ref[...] = gain_ref[...].reshape(1, width)[:, j * depth : (j + 1) * depth]

    strand_rows = pl.ds(pl.multiple_of(c * 64, 64), 64)

    def make_act(slot):
        line = jnp.concatenate([tok_buf[slot, 0], tok_buf[slot, 1], tok_buf[slot, 2]], axis=1)
        wide = jnp.broadcast_to(line, (TAP_ROWS, 3 * rows))
        start = rows - DILATION_STEP - taps // 2 + TAP_ROWS - 1
        turned = pltpu.roll(wide, 3 * rows - start, 1, stride=1, stride_axis=0)[:, :span]
        place = lax.broadcasted_iota(jnp.int32, (TAP_ROWS, span), 1) + s * rows - DILATION_STEP
        turned = jnp.where((place >= 0) & (place < seq * rows), turned, 4)
        onehot = jnp.concatenate([jnp.where(turned == kind, 1.0, 0.0) for kind in range(4)], axis=0)
        low = onehot.astype(jnp.bfloat16)
        hot[...] = low
        total = jnp.zeros((1, span), jnp.float32)
        step = 256
        for at in range(0, width, step):
            e = dot_rows(table_ref[strand_rows, at : at + step], low)
            total = total + jnp.sum(e * e, axis=0, keepdims=True)
        scale = lax.rsqrt(total * (1.0 / width) + 1e-06)
        scale_high = scale.astype(jnp.bfloat16).astype(jnp.float32)
        scaled[0:64] = (onehot * scale_high).astype(jnp.bfloat16)
        scaled[64:128] = (onehot * (scale - scale_high)).astype(jnp.bfloat16)

    def act_block(at, size):
        z = dot_rows(scaled[:, at : at + size], local_table_ref[...])
        act[at : at + size, :] = gelu(z * local_gain_ref[...]).astype(jnp.bfloat16)

    def conv_block(at, size):
        total = jnp.zeros((size, inner), jnp.float32)
        for k in range(3):
            tap = jnp.where(c == 1, 2 - k, k)
            total = total + jnp.dot(
                act[at + k * DILATION_STEP : at + k * DILATION_STEP + size, :], conv_buf[tap],
                preferred_element_type=jnp.float32,
            )
        return total

    def part_copy(off, piece):
        j = lax.rem(d + off, dp)
        return pltpu.make_async_remote_copy(
            src_ref=send_buf.at[off - 1, piece], dst_ref=recv_buf.at[off - 1, piece],
            send_sem=part_send.at[off - 1, piece], recv_sem=part_recv.at[off - 1, piece],
            device_id=(g, s, j, c), device_id_type=MESH,
        )

    big = DILATION_STEP
    for off in range(1, dp):
        tok_wait(dp - off)
        make_act(dp - off)
        for at in range(0, 2 * DILATION_STEP, big):
            act_block(at, big)
        if off == 1:
            load_conv.wait()
        for at in range(0, rows, big):
            act_block(at + 2 * DILATION_STEP, big)
            total = conv_block(at, big).astype(jnp.bfloat16)
            for piece in range(at // PIECE, (at + big) // PIECE):
                send_buf[off - 1, piece] = total[piece * PIECE - at : piece * PIECE - at + PIECE]
                part_copy(off, piece).start()

    tok_wait(0)
    make_act(0)
    for at in range(0, 2 * DILATION_STEP, big):
        act_block(at, big)
    for off in range(1, dp):
        point_copy(off).wait_recv()
        for goff in range(1, groups):
            pass_copy(off, goff).start()
    for at in range(0, rows, big):
        act_block(at + 2 * DILATION_STEP, big)
    if dp == 1:
        load_conv.wait()
    own[...] = conv_block(0, rows)

    load_point.wait()
    for off in range(1, dp):
        for goff in range(1, groups):
            source = lax.rem(d + dp - off, dp)
            from_group = lax.rem(g + groups - goff, groups)
            block = point_buf.at[pl.ds(pl.multiple_of(source * point_rows + from_group * share, 16), share)]
            pltpu.make_async_remote_copy(
                src_ref=block, dst_ref=block,
                send_sem=fwd_send.at[off - 1, goff - 1], recv_sem=fwd_recv.at[off - 1, goff - 1],
                device_id=(lax.rem(g + goff, groups), s, d, c), device_id_type=MESH,
            ).wait_recv()

    def mid_copy(piece):
        return pltpu.make_async_remote_copy(
            src_ref=mid.at[piece], dst_ref=mid_in.at[piece],
            send_sem=mid_send.at[piece], recv_sem=mid_recv.at[piece],
            device_id=(g, s, d, 1 - c), device_id_type=MESH,
        )

    def out_copy(piece):
        block = pl.ds(piece * PIECE, PIECE)
        return pltpu.make_async_copy(out_buf.at[block], out_ref.at[0, block], out_sem.at[piece])

    def finish(piece):
        at = piece * PIECE
        lanes = hot[:, DILATION_STEP + at : DILATION_STEP + at + PIECE]
        e = dot_rows(jnp.concatenate([lanes, lanes], axis=0), table_ref[:, col])
        mid_copy(piece).wait_recv()
        both = (mid[piece].astype(jnp.float32) + mid_in[piece].astype(jnp.float32)).astype(jnp.bfloat16)
        branch = jnp.dot(both, point_buf[...], preferred_element_type=jnp.float32)
        out_buf[at : at + PIECE, :] = ((e + branch) * 0.5).astype(jnp.bfloat16)
        out_copy(piece).start()

    for piece in range(pieces):
        x = own[piece * PIECE : (piece + 1) * PIECE]
        for off in range(1, dp):
            part_copy(off, piece).wait_recv()
            x = x + recv_buf[off - 1, piece].astype(jnp.float32)
        scale = lax.rsqrt(jnp.mean(x * x, axis=1, keepdims=True) + 1e-06)
        mid[piece] = gelu(x * scale * gain_mid_ref[...].reshape(1, inner)).astype(jnp.bfloat16)
        mid_copy(piece).start()
        if piece:
            finish(piece - 1)
    finish(pieces - 1)

    for off in range(dp):
        tok_each(off, lambda o, p: tok_copy(o, p).wait_send())
    for off in range(1, dp):
        point_copy(off).wait_send()
        for goff in range(1, groups):
            pass_copy(off, goff).wait_send()
        for piece in range(pieces):
            part_copy(off, piece).wait_send()
    for piece in range(pieces):
        mid_copy(piece).wait_send()
        out_copy(piece).wait()


def per_device(counts, tokens, stem_table, conv_weight, gain_in, gain_mid, point_weight):
    groups, seq, dp = counts
    rows = tokens.shape[1]
    taps, kinds, width = stem_table.shape
    depth, inner = conv_weight.shape[1:]
    half = width // 2
    pieces = rows // PIECE
    span = rows + 2 * DILATION_STEP
    vmem = pl.BlockSpec(memory_space=pltpu.VMEM)
    anywhere = pl.BlockSpec(memory_space=pltpu.HBM)
    dma = pltpu.SemaphoreType.DMA
    bf16 = jnp.bfloat16
    others, passes = max(dp - 1, 1), max(groups - 1, 1)
    return pl.pallas_call(
        functools.partial(kernel, counts),
        out_shape=jax.ShapeDtypeStruct((1, rows, half), bf16),
        in_specs=[vmem] * 4 + [anywhere] * 2,
        out_specs=anywhere,
        scratch_shapes=[
            pltpu.VMEM((64, width), jnp.float32),
            pltpu.VMEM((128, width), bf16),
            pltpu.VMEM((128, depth), bf16),
            pltpu.VMEM((1, depth), jnp.float32),
            pltpu.VMEM((dp, 3, 1, rows), jnp.int32),
            pltpu.VMEM((64, span), bf16),
            pltpu.VMEM((128, span), bf16),
            pltpu.VMEM((span, depth), bf16),
            pltpu.VMEM((3, depth, inner), bf16),
            pltpu.VMEM((inner, half), bf16),
            pltpu.VMEM((others, pieces, PIECE, inner), bf16),
            pltpu.VMEM((others, pieces, PIECE, inner), bf16),
            pltpu.VMEM((rows, inner), jnp.float32),
            pltpu.VMEM((pieces, PIECE, inner), bf16),
            pltpu.VMEM((pieces, PIECE, inner), bf16),
            dma((dp, 3)), dma((dp, 3)), dma, dma,
            dma((others,)), dma((others,)), dma((others, passes)), dma((others, passes)),
            dma((others, pieces)), dma((others, pieces)), dma((pieces,)), dma((pieces,)),
            pltpu.VMEM((rows, half), bf16), dma((pieces,)),
        ],
        compiler_params=pltpu.CompilerParams(
            collective_id=0, has_side_effects=True, vmem_limit_bytes=60 * 1024 * 1024
        ),
        cost_estimate=pl.CostEstimate(
            flops=2 * rows * inner * (3 * width + width), bytes_accessed=8 * 2**20,
            transcendentals=rows * width,
        ),
    )(tokens, stem_table, gain_in, gain_mid, conv_weight, point_weight)


def solution(mesh):
    counts = tuple(mesh.shape[name] for name in ("groups", "seq", "dp"))
    return jax.shard_map(
        functools.partial(per_device, counts),
        mesh=mesh,
        in_specs=(P(("groups", "dp"), "seq"), P(), P(None, "dp", None), P(), P(), P("dp", None)),
        out_specs=P(("groups", "dp"), "seq", "strand"),
        check_vma=False,
    )
```

```python
import functools

import jax
import jax.numpy as jnp
from jax import lax
from jax.experimental import pallas as pl
from jax.experimental.pallas import tpu as pltpu
from jax.sharding import PartitionSpec as P

DILATION_STEP = 256
TAP_ROWS = 16
PIECE = 64
MESH = pl.DeviceIdType.MESH


def gelu(x):
    inner = x * (0.7978845608028654 + 0.035677408136300125 * (x * x))
    half = 0.5 * x
    return half + half * jnp.tanh(inner)


def dot_rows(a, b):
    return lax.dot_general(a, b, (((0,), (0,)), ((), ())), preferred_element_type=jnp.float32)


def kernel(
    counts, tok_ref, stem_ref, gain_ref, gain_mid_ref, conv_ref, point_ref, out_ref,
    stem_buf, table_ref, local_table_ref, local_gain_ref, tok_buf, hot, scaled, act, conv_buf, point_buf, send_buf, recv_buf, own, mid, mid_in,
    tok_send, tok_recv, load_sem, point_load_sem, point_send, point_recv, fwd_send, fwd_recv,
    part_send, part_recv, mid_send, mid_recv, out_buf, out_sem,
):
    groups, seq, dp = counts
    rows = tok_ref.shape[1]
    taps, kinds, width = stem_ref.shape
    depth = conv_ref.shape[1]
    inner = conv_ref.shape[2]
    point_rows = point_ref.shape[0]
    half = width // 2
    span = rows + 2 * DILATION_STEP
    pieces = rows // PIECE
    g = lax.axis_index("groups")
    s = lax.axis_index("seq")
    d = lax.axis_index("dp")
    c = lax.axis_index("strand")

    load_conv = pltpu.make_async_copy(conv_ref, conv_buf, load_sem)
    load_conv.start()
    col = pl.ds(pl.multiple_of(c * half, 128), half)
    load_point = pltpu.make_async_copy(
        point_ref.at[:, col], point_buf.at[pl.ds(pl.multiple_of(d * point_rows, 16), point_rows)], point_load_sem
    )
    load_point.start()

    barrier = pltpu.get_barrier_semaphore()

    def greet(target):
        pl.semaphore_signal(barrier, inc=1, device_id=target, device_id_type=MESH)

    for off in range(dp):
        j = lax.rem(d + off, dp)
        if off:
            greet((g, s, j, c))

        @pl.when(s > 0)
        def _():
            greet((g, s - 1, j, c))

        @pl.when(s < seq - 1)
        def _():
            greet((g, s + 1, j, c))

    greet((g, s, d, 1 - c))
    for goff in range(1, groups):
        greet((lax.rem(g + goff, groups), s, d, c))
    sides = 1 + (s > 0).astype(jnp.int32) + (s < seq - 1).astype(jnp.int32)
    pl.semaphore_wait(barrier, dp * sides - 1 + 1 + groups - 1)

    def tok_copy(off, place):
        j = lax.rem(d + off, dp)
        return pltpu.make_async_remote_copy(
            src_ref=tok_ref, dst_ref=tok_buf.at[off, 2 - place],
            send_sem=tok_send.at[off, 2 - place], recv_sem=tok_recv.at[off, 2 - place],
            device_id=(g, s + place - 1, j, c), device_id_type=MESH,
        )

    def tok_each(off, action):
        @pl.when(s > 0)
        def _():
            action(off, 0)

        @pl.when(s < seq - 1)
        def _():
            action(off, 2)

        if off:
            action(off, 1)

    for off in list(range(1, dp)) + [0]:
        tok_each(off, lambda o, p: tok_copy(o, p).start())
    tok_buf[0, 1] = tok_ref[...]
    for off in range(dp):
        @pl.when(s == 0)
        def _():
            tok_buf[off, 0] = jnp.full((1, rows), 4, jnp.int32)

        @pl.when(s == seq - 1)
        def _():
            tok_buf[off, 2] = jnp.full((1, rows), 4, jnp.int32)

    share = point_rows // groups

    def point_copy(off):
        j = lax.rem(d + off, dp)
        return pltpu.make_async_remote_copy(
            src_ref=point_ref.at[pl.ds(pl.multiple_of(g * share, 16), share), col],
            dst_ref=point_buf.at[pl.ds(pl.multiple_of(d * point_rows + g * share, 16), share)],
            send_sem=point_send.at[off - 1], recv_sem=point_recv.at[off - 1],
            device_id=(g, s, j, c), device_id_type=MESH,
        )

    def pass_copy(off, goff):
        source = lax.rem(d + dp - off, dp)
        block = point_buf.at[pl.ds(pl.multiple_of(source * point_rows + g * share, 16), share)]
        return pltpu.make_async_remote_copy(
            src_ref=block, dst_ref=block,
            send_sem=fwd_send.at[off - 1, goff - 1], recv_sem=fwd_recv.at[off - 1, goff - 1],
            device_id=(lax.rem(g + goff, groups), s, d, c), device_id_type=MESH,
        )

    for off in range(1, dp):
        point_copy(off).start()

    def tok_wait(off):
        def wait_from(o, p):
            pltpu.make_async_remote_copy(
                src_ref=tok_ref, dst_ref=tok_buf.at[o, p],
                send_sem=tok_send.at[o, p], recv_sem=tok_recv.at[o, p],
                device_id=(g, s, d, 1 - c), device_id_type=MESH,
            ).wait_recv()

        tok_each(off, wait_from)

    stem_buf[...] = jnp.zeros_like(stem_buf)
    for tap in range(taps):
        stem_buf[tap * kinds : (tap + 1) * kinds] = stem_ref[tap].astype(jnp.float32)
    row = lax.broadcasted_iota(jnp.int32, (128, 64), 0)
    source = lax.broadcasted_iota(jnp.int32, (128, 64), 1)
    place = row % TAP_ROWS
    kind = (row // TAP_ROWS) % kinds
    ahead = kinds * (TAP_ROWS - 1 - place) + kind
    behind = kinds * (place - 1) + kinds - 1 - kind
    pick = (source == jnp.where(row < 64, ahead, behind)) & (place > 0)
    pick = jnp.where(pick, 1.0, 0.0).astype(jnp.bfloat16)
    table_ref[...] = jnp.dot(
        pick, stem_buf[...].astype(jnp.bfloat16), preferred_element_type=jnp.float32
    ).astype(jnp.bfloat16)
    strand_rows = pl.ds(pl.multiple_of(c * 64, 64), 64)
    for j in range(dp):
        @pl.when(d == j)
        def _():
            block = table_ref[strand_rows, j * depth : (j + 1) * depth]
            local_table_ref[0:64] = block
            local_table_ref[64:128] = block
            local_gain_ref[...] = gain_ref[...].reshape(1, width)[:, j * depth : (j + 1) * depth]

    strand_rows = pl.ds(pl.multiple_of(c * 64, 64), 64)

    def make_act(slot):
        line = jnp.concatenate([tok_buf[slot, 0], tok_buf[slot, 1], tok_buf[slot, 2]], axis=1)
        wide = jnp.broadcast_to(line, (TAP_ROWS, 3 * rows))
        start = rows - DILATION_STEP - taps // 2 + TAP_ROWS - 1
        turned = pltpu.roll(wide, 3 * rows - start, 1, stride=1, stride_axis=0)[:, :span]
        place = lax.broadcasted_iota(jnp.int32, (TAP_ROWS, span), 1) + s * rows - DILATION_STEP
        turned = jnp.where((place >= 0) & (place < seq * rows), turned, 4)
        onehot = jnp.concatenate([jnp.where(turned == kind, 1.0, 0.0) for kind in range(4)], axis=0)
        low = onehot.astype(jnp.bfloat16)
        hot[...] = low
        total = jnp.zeros((1, span), jnp.float32)
        step = 256
        for at in range(0, width, step):
            e = dot_rows(table_ref[strand_rows, at : at + step], low)
            total = total + jnp.sum(e * e, axis=0, keepdims=True)
        scale = lax.rsqrt(total * (1.0 / width) + 1e-06)
        scale_high = scale.astype(jnp.bfloat16).astype(jnp.float32)
        scaled[0:64] = (onehot * scale_high).astype(jnp.bfloat16)
        scaled[64:128] = (onehot * (scale - scale_high)).astype(jnp.bfloat16)

    def act_block(at, size):
        z = dot_rows(scaled[:, at : at + size], local_table_ref[...])
        act[at : at + size, :] = gelu(z * local_gain_ref[...]).astype(jnp.bfloat16)

    def conv_block(at, size):
        total = jnp.zeros((size, inner), jnp.float32)
        for k in range(3):
            tap = jnp.where(c == 1, 2 - k, k)
            total = total + jnp.dot(
                act[at + k * DILATION_STEP : at + k * DILATION_STEP + size, :], conv_buf[tap],
                preferred_element_type=jnp.float32,
            )
        return total

    def part_copy(off, piece):
        j = lax.rem(d + off, dp)
        return pltpu.make_async_remote_copy(
            src_ref=send_buf.at[off - 1, piece], dst_ref=recv_buf.at[off - 1, piece],
            send_sem=part_send.at[off - 1, piece], recv_sem=part_recv.at[off - 1, piece],
            device_id=(g, s, j, c), device_id_type=MESH,
        )

    big = DILATION_STEP
    load_conv.wait()
    for off in range(1, dp):
        tok_wait(dp - off)
        make_act(dp - off)
        for at in range(0, 2 * DILATION_STEP, big):
            act_block(at, big)
        for at in range(0, rows, big):
            act_block(at + 2 * DILATION_STEP, big)
            total = conv_block(at, big).astype(jnp.bfloat16)
            for piece in range(at // PIECE, (at + big) // PIECE):
                send_buf[off - 1, piece] = total[piece * PIECE - at : piece * PIECE - at + PIECE]
                part_copy(off, piece).start()

    tok_wait(0)
    make_act(0)
    for at in range(0, 2 * DILATION_STEP, big):
        act_block(at, big)
    for off in range(1, dp):
        point_copy(off).wait_recv()
        for goff in range(1, groups):
            pass_copy(off, goff).start()
    for at in range(0, rows, big):
        act_block(at + 2 * DILATION_STEP, big)
        own[at : at + big] = conv_block(at, big)

    load_point.wait()
    for off in range(1, dp):
        for goff in range(1, groups):
            source = lax.rem(d + dp - off, dp)
            from_group = lax.rem(g + groups - goff, groups)
            block = point_buf.at[pl.ds(pl.multiple_of(source * point_rows + from_group * share, 16), share)]
            pltpu.make_async_remote_copy(
                src_ref=block, dst_ref=block,
                send_sem=fwd_send.at[off - 1, goff - 1], recv_sem=fwd_recv.at[off - 1, goff - 1],
                device_id=(lax.rem(g + goff, groups), s, d, c), device_id_type=MESH,
            ).wait_recv()

    def mid_copy(piece):
        return pltpu.make_async_remote_copy(
            src_ref=mid.at[piece], dst_ref=mid_in.at[piece],
            send_sem=mid_send.at[piece], recv_sem=mid_recv.at[piece],
            device_id=(g, s, d, 1 - c), device_id_type=MESH,
        )

    def out_copy(piece):
        block = pl.ds(piece * PIECE, PIECE)
        return pltpu.make_async_copy(out_buf.at[block], out_ref.at[0, block], out_sem.at[piece])

    def finish(piece):
        at = piece * PIECE
        lanes = hot[:, DILATION_STEP + at : DILATION_STEP + at + PIECE]
        e = dot_rows(jnp.concatenate([lanes, lanes], axis=0), table_ref[:, col])
        mid_copy(piece).wait_recv()
        both = (mid[piece].astype(jnp.float32) + mid_in[piece].astype(jnp.float32)).astype(jnp.bfloat16)
        branch = jnp.dot(both, point_buf[...], preferred_element_type=jnp.float32)
        out_buf[at : at + PIECE, :] = ((e + branch) * 0.5).astype(jnp.bfloat16)
        out_copy(piece).start()

    for piece in range(pieces):
        x = own[piece * PIECE : (piece + 1) * PIECE]
        for off in range(1, dp):
            part_copy(off, piece).wait_recv()
            x = x + recv_buf[off - 1, piece].astype(jnp.float32)
        scale = lax.rsqrt(jnp.mean(x * x, axis=1, keepdims=True) + 1e-06)
        mid[piece] = gelu(x * scale * gain_mid_ref[...].reshape(1, inner)).astype(jnp.bfloat16)
        mid_copy(piece).start()
        if piece:
            finish(piece - 1)
    finish(pieces - 1)

    for off in range(dp):
        tok_each(off, lambda o, p: tok_copy(o, p).wait_send())
    for off in range(1, dp):
        point_copy(off).wait_send()
        for goff in range(1, groups):
            pass_copy(off, goff).wait_send()
        for piece in range(pieces):
            part_copy(off, piece).wait_send()
    for piece in range(pieces):
        mid_copy(piece).wait_send()
        out_copy(piece).wait()


def per_device(counts, tokens, stem_table, conv_weight, gain_in, gain_mid, point_weight):
    groups, seq, dp = counts
    rows = tokens.shape[1]
    taps, kinds, width = stem_table.shape
    depth, inner = conv_weight.shape[1:]
    half = width // 2
    pieces = rows // PIECE
    span = rows + 2 * DILATION_STEP
    vmem = pl.BlockSpec(memory_space=pltpu.VMEM)
    anywhere = pl.BlockSpec(memory_space=pltpu.HBM)
    dma = pltpu.SemaphoreType.DMA
    bf16 = jnp.bfloat16
    others, passes = max(dp - 1, 1), max(groups - 1, 1)
    return pl.pallas_call(
        functools.partial(kernel, counts),
        out_shape=jax.ShapeDtypeStruct((1, rows, half), bf16),
        in_specs=[vmem] * 4 + [anywhere] * 2,
        out_specs=anywhere,
        scratch_shapes=[
            pltpu.VMEM((64, width), jnp.float32),
            pltpu.VMEM((128, width), bf16),
            pltpu.VMEM((128, depth), bf16),
            pltpu.VMEM((1, depth), jnp.float32),
            pltpu.VMEM((dp, 3, 1, rows), jnp.int32),
            pltpu.VMEM((64, span), bf16),
            pltpu.VMEM((128, span), bf16),
            pltpu.VMEM((span, depth), bf16),
            pltpu.VMEM((3, depth, inner), bf16),
            pltpu.VMEM((inner, half), bf16),
            pltpu.VMEM((others, pieces, PIECE, inner), bf16),
            pltpu.VMEM((others, pieces, PIECE, inner), bf16),
            pltpu.VMEM((rows, inner), jnp.float32),
            pltpu.VMEM((pieces, PIECE, inner), bf16),
            pltpu.VMEM((pieces, PIECE, inner), bf16),
            dma((dp, 3)), dma((dp, 3)), dma, dma,
            dma((others,)), dma((others,)), dma((others, passes)), dma((others, passes)),
            dma((others, pieces)), dma((others, pieces)), dma((pieces,)), dma((pieces,)),
            pltpu.VMEM((rows, half), bf16), dma((pieces,)),
        ],
        compiler_params=pltpu.CompilerParams(
            collective_id=0, has_side_effects=True, vmem_limit_bytes=60 * 1024 * 1024
        ),
        cost_estimate=pl.CostEstimate(
            flops=2 * rows * inner * (3 * width + width), bytes_accessed=8 * 2**20,
            transcendentals=rows * width,
        ),
    )(tokens, stem_table, gain_in, gain_mid, conv_weight, point_weight)


def solution(mesh):
    counts = tuple(mesh.shape[name] for name in ("groups", "seq", "dp"))
    return jax.shard_map(
        functools.partial(per_device, counts),
        mesh=mesh,
        in_specs=(P(("groups", "dp"), "seq"), P(), P(None, "dp", None), P(), P(), P("dp", None)),
        out_specs=P(("groups", "dp"), "seq", "strand"),
        check_vma=False,
    )
```
